128 devices in a mesh: dp: 8 (over z_hi, y), seq: 16 (over z_lo, x, core).
Axes of the slice: x: 4, y: 4, z: 4 (z_hi: 2, z_lo: 2; z = z_hi * 2 + z_lo), core: 2. Of those that a mesh axis runs over, the one named last changes fastest.
Arguments:
- queries: bfloat16 [8, 2048, 2048], P('dp', 'seq'), may hold values from -10 to 10
- keys: bfloat16 [8, 2048, 2048], P('dp', 'seq'), may hold values from -10 to 10
- values: bfloat16 [8, 2048, 2048], P('dp', 'seq'), may hold values from -6 to 6
- out_weight: bfloat16 [2048, 2048], replicated, may hold values from -0.125 to 0.125
- out_grad: bfloat16 [8, 2048, 2048], P('dp', 'seq'), may hold values from -6 to 6
Outputs:
- layer_out: bfloat16 [8, 2048, 2048], P('dp', 'seq')
- grad_queries: bfloat16 [8, 2048, 2048], P('dp', 'seq')
- grad_keys: bfloat16 [8, 2048, 2048], P('dp', 'seq')
- grad_values: bfloat16 [8, 2048, 2048], P('dp', 'seq')
- grad_weight: float32 [2048, 2048], P('seq')
The draws below stay inside these ranges and needn't reach their ends.
All inputs are finite; a program needn't handle non-finite values.
Results may differ from the reference program's by a relative error of at most 0.035.
Values may be sent and summed in bfloat16 or wider, within the bound.
No kernel may reach another device: no remote copies, remote signals or barrier semaphores. Data moves between devices by JAX's collectives and lax.ppermute only.
A program may use at most 192 MiB of HBM per device.

```python
import jax
import jax.numpy as jnp
from jax import lax

D = 2048
HEADS = 16
HEAD_DIM = 128
SEQS = 8
LENGTH = 2048


def clipped_noise(key):
    return jnp.clip(jax.random.normal(jax.random.fold_in(key, 1), (SEQS, LENGTH, D), jnp.float32), -4.0, 4.0)


def draw_queries(key, part):
    key = jax.random.fold_in(key, 11)
    noise = clipped_noise(key)
    return noise.astype(jnp.bfloat16)


def draw_keys(key, part):
    key = jax.random.fold_in(key, 23)
    noise = clipped_noise(key)
    return noise.astype(jnp.bfloat16)


def steps_of(own_key, extent, cuts, low, top_value):
    level = 1.0
    for position, parts in cuts:
        heights = jax.random.uniform(jax.random.fold_in(jax.random.fold_in(own_key, 6), position), (parts,), jnp.float32, low / len(cuts), top_value / len(cuts))
        level = level * jnp.repeat(jnp.exp(heights), extent[position] // parts).reshape((-1,) + (1,) * (len(extent) - 1 - position))
    return level


def normal_values(own_key, dims, spread, most, pieces=(), held_as=jnp.bfloat16):
    gain = steps_of(own_key, dims, pieces, -0.22, 0.18) if pieces else 1.0
    values = jax.random.normal(own_key, dims, jnp.float32) * spread * gain
    return jnp.minimum(jnp.maximum(values, -most), most).astype(held_as)


def setup_inputs(seed: int = 0) -> dict:
    key_list = jax.random.split(jax.random.key(seed), 6)
    return {
        "queries": draw_queries(jax.random.fold_in(key_list[5], 71), 0),
        "keys": draw_keys(jax.random.fold_in(key_list[5], 71), 0),
        "values": normal_values(key_list[2], (SEQS, LENGTH, D), 1.0, 6.0, ((0, 8), (1, 16))),
        "out_weight": normal_values(key_list[3], (D, D), D ** -0.5, 0.125),
        "out_grad": normal_values(key_list[4], (SEQS, LENGTH, D), 1.0, 6.0, ((0, 8), (1, 16))),
    }


def probabilities(query_head, key_head, factor):
    scores = jnp.dot(query_head, key_head.T, preferred_element_type=jnp.float32) * factor
    row_ids = jnp.arange(LENGTH)[:, None]
    col_ids = jnp.arange(LENGTH)[None, :]
    visible = row_ids >= col_ids
    scores = jnp.where(visible, scores, -1e30)
    peak = jnp.max(scores, axis=1, keepdims=True)
    weights = jnp.where(visible, jnp.exp(scores - peak), 0.0)
    return weights / jnp.sum(weights, axis=1, keepdims=True)


def split_heads(array):
    return array.reshape(SEQS, LENGTH, HEADS, HEAD_DIM).transpose(0, 2, 1, 3).reshape(SEQS * HEADS, LENGTH, HEAD_DIM)


def join_heads(array):
    return array.reshape(SEQS, HEADS, LENGTH, HEAD_DIM).transpose(0, 2, 1, 3).reshape(SEQS, LENGTH, D)


def reference(queries, keys, values, out_weight, out_grad):
    factor = HEAD_DIM ** -0.5
    q_split = split_heads(queries)
    k_split = split_heads(keys)
    v_split = split_heads(values)

    def forward(items):
        query_head, key_head, value_head = items
        weights = probabilities(query_head, key_head, factor).astype(jnp.bfloat16)
        return jnp.dot(weights, value_head, preferred_element_type=jnp.float32).astype(jnp.bfloat16)

    attn_heads = lax.map(forward, (q_split, k_split, v_split))
    attn = join_heads(attn_heads)
    attn_rows = attn.reshape(SEQS * LENGTH, D)
    grad_rows = out_grad.reshape(SEQS * LENGTH, D)
    layer_out = jnp.dot(attn_rows, out_weight, preferred_element_type=jnp.float32).astype(jnp.bfloat16)
    grad_weight = jnp.dot(attn_rows.T, grad_rows, preferred_element_type=jnp.float32)
    d_attn = jnp.dot(grad_rows, out_weight.T, preferred_element_type=jnp.float32).astype(jnp.bfloat16)
    d_split = split_heads(d_attn.reshape(SEQS, LENGTH, D))

    def backward(items):
        query_head, key_head, value_head, attn_head, d_head = items
        probs_f = probabilities(query_head, key_head, factor)
        probs = probs_f.astype(jnp.bfloat16)
        d_probs = jnp.dot(d_head, value_head.T, preferred_element_type=jnp.float32)
        delta = jnp.sum(d_head.astype(jnp.float32) * attn_head.astype(jnp.float32), axis=1, keepdims=True)
        d_scores = (probs_f * (d_probs - delta)).astype(jnp.bfloat16)
        grad_v = jnp.dot(probs.T, d_head, preferred_element_type=jnp.float32).astype(jnp.bfloat16)
        grad_q = (jnp.dot(d_scores, key_head, preferred_element_type=jnp.float32) * factor).astype(jnp.bfloat16)
        grad_k = (jnp.dot(d_scores.T, query_head, preferred_element_type=jnp.float32) * factor).astype(jnp.bfloat16)
        return grad_q, grad_k, grad_v

    grad_q, grad_k, grad_v = lax.map(backward, (q_split, k_split, v_split, attn_heads, d_split))
    return (layer_out.reshape(SEQS, LENGTH, D), join_heads(grad_q), join_heads(grad_k), join_heads(grad_v), grad_weight)
```

```python
import math

import jax
import jax.numpy as jnp
from jax import lax
from jax.experimental import pallas as pl
from jax.experimental.pallas import tpu as pltpu
from jax.sharding import PartitionSpec as P

B16 = jnp.bfloat16
F32 = jnp.float32
HEAD = 128
TOK = 128
LENGTH = 2048
WIDTH = 2048
HEADS = 16
BLOCK = 256
BLOCKS = LENGTH // BLOCK
FACTOR = HEAD ** (-0.5)
FACTOR2 = FACTOR * math.log2(math.e)
VMEM_LIMIT = 48 * 1024 * 1024

ZN, XN, CN, YN, HN = 2, 4, 2, 4, 2


def nt(a, b):
    return lax.dot_general(a, b, (((1,), (1,)), ((), ())), preferred_element_type=F32)


def nn(a, b):
    return lax.dot_general(a, b, (((1,), (0,)), ((), ())), preferred_element_type=F32)


def params():
    return pltpu.CompilerParams(vmem_limit_bytes=VMEM_LIMIT)


def cost(flops, nbytes, exps=0):
    return pl.CostEstimate(flops=flops, bytes_accessed=nbytes, transcendentals=exps)


def pack_kernel(q_ref, k_ref, v_ref, g_ref, w_ref, out_ref):
    d = nt(g_ref[...], w_ref[...]).astype(B16)
    for h in range(2):
        cols = slice(h * HEAD, (h + 1) * HEAD)
        out_ref[h, 0] = q_ref[:, cols]
        out_ref[h, 1] = k_ref[:, cols]
        out_ref[h, 2] = v_ref[:, cols]
        out_ref[h, 3] = d[:, cols]


def pack(q, k, v, g, w):
    part = pl.BlockSpec((TOK, 2 * HEAD), lambda i: (0, i))
    return pl.pallas_call(
        pack_kernel,
        grid=(HEADS // 2,),
        in_specs=[
            part,
            part,
            part,
            pl.BlockSpec((TOK, WIDTH), lambda i: (0, 0)),
            pl.BlockSpec((2 * HEAD, WIDTH), lambda i: (i, 0)),
        ],
        out_specs=pl.BlockSpec((2, 4, TOK, HEAD), lambda i: (i, 0, 0, 0)),
        out_shape=jax.ShapeDtypeStruct((HEADS, 4, TOK, HEAD), B16),
        compiler_params=params(),
        cost_estimate=cost(2 * TOK * WIDTH * WIDTH, 12 << 20),
        name="pack",
    )(q, k, v, g, w)


def rows_of(ref, which, first, count):
    return jnp.concatenate(
        [ref[t, which] for t in range(first // TOK, (first + count) // TOK)], axis=0
    )


def mask_of():
    key = lax.broadcasted_iota(jnp.int32, (BLOCK, BLOCK), 0)
    query = lax.broadcasted_iota(jnp.int32, (BLOCK, BLOCK), 1)
    return query >= key


def forward_kernel(pos_ref, x_ref, o_ref, keep_ref, send_ref, stat_ref, vt_ref):
    core = pos_ref[2]
    visible = mask_of()
    for t in range(HEADS):
        vt_ref[:, t * TOK : (t + 1) * TOK] = x_ref[t, 2].T
    for j in range(BLOCKS):
        first = j * BLOCK
        q = rows_of(x_ref, 0, first, BLOCK)
        tiles = []
        for i in range(j + 1):
            s = nt(rows_of(x_ref, 1, i * BLOCK, BLOCK), q) * FACTOR2
            tiles.append(jnp.where(visible, s, -1e30) if i == j else s)
        top = tiles[0]
        for s in tiles[1:]:
            top = jnp.maximum(top, s)
        top = jnp.max(top, axis=0, keepdims=True)
        total = None
        acc = None
        for i, s in enumerate(tiles):
            p = jnp.exp2(s - top)
            total = p if total is None else total + p
            term = nn(vt_ref[:, i * BLOCK : (i + 1) * BLOCK], p.astype(B16))
            acc = term if acc is None else acc + term
        total = jnp.sum(total, axis=0, keepdims=True)
        ot = acc * (1.0 / total)
        ob = ot.astype(B16)
        oc = ot.T.astype(B16)
        o_ref[2 * j] = oc[:TOK]
        o_ref[2 * j + 1] = oc[TOK:]
        keep_ref[j] = jnp.where(core == 0, ob[:, :TOK], ob[:, TOK:])
        send_ref[j] = jnp.where(core == 0, ob[:, TOK:], ob[:, :TOK])
        d = rows_of(x_ref, 3, first, BLOCK)
        delta = jnp.sum(d.T.astype(F32) * ob.astype(F32), axis=0, keepdims=True)
        stat_ref[0:1, first : first + BLOCK] = top + jnp.log2(total)
        stat_ref[1:2, first : first + BLOCK] = delta


def forward(pos, x):
    vmem = pl.BlockSpec(memory_space=pltpu.VMEM)
    return pl.pallas_call(
        forward_kernel,
        in_specs=[pl.BlockSpec(memory_space=pltpu.SMEM), vmem],
        out_specs=[vmem, vmem, vmem, vmem],
        out_shape=[
            jax.ShapeDtypeStruct((HEADS, TOK, HEAD), B16),
            jax.ShapeDtypeStruct((BLOCKS, HEAD, TOK), B16),
            jax.ShapeDtypeStruct((BLOCKS, HEAD, TOK), B16),
            jax.ShapeDtypeStruct((8, LENGTH), F32),
        ],
        scratch_shapes=[pltpu.VMEM((HEAD, LENGTH), B16)],
        compiler_params=params(),
        cost_estimate=cost(4 * LENGTH * LENGTH * HEAD, 4 << 20, LENGTH * LENGTH // 2),
        name="attention_forward",
    )(pos, x)


def backward_kernel(x_ref, stat_ref, out_ref, dqt_ref):
    visible = mask_of()
    dqt_ref[...] = jnp.zeros_like(dqt_ref)
    for i in range(BLOCKS):
        first = i * BLOCK
        k = rows_of(x_ref, 1, first, BLOCK)
        v = rows_of(x_ref, 2, first, BLOCK)
        kt = k.T
        dk = None
        dv = None
        for j in range(i, BLOCKS):
            cols = slice(j * BLOCK, (j + 1) * BLOCK)
            q = rows_of(x_ref, 0, j * BLOCK, BLOCK)
            d = rows_of(x_ref, 3, j * BLOCK, BLOCK)
            s = nt(k, q) * FACTOR2 - stat_ref[0:1, cols]
            if i == j:
                s = jnp.where(visible, s, -1e30)
            p = jnp.exp2(s)
            dp = nt(v, d) - stat_ref[1:2, cols]
            ds = (p * dp).astype(B16)
            term = nn(p.astype(B16), d)
            dv = term if dv is None else dv + term
            term = nn(ds, q)
            dk = term if dk is None else dk + term
            dqt_ref[:, cols] += nn(kt, ds)
        dk = (dk * FACTOR).astype(B16)
        dv = dv.astype(B16)
        for t in range(2):
            rows = slice(t * TOK, (t + 1) * TOK)
            out_ref[2 * i + t, 1] = dk[rows]
            out_ref[2 * i + t, 2] = dv[rows]
    for t in range(HEADS):
        part = dqt_ref[:, t * TOK : (t + 1) * TOK] * FACTOR
        out_ref[t, 0] = part.T.astype(B16)


def backward(x, stat):
    vmem = pl.BlockSpec(memory_space=pltpu.VMEM)
    return pl.pallas_call(
        backward_kernel,
        in_specs=[vmem, vmem],
        out_specs=vmem,
        out_shape=jax.ShapeDtypeStruct((HEADS, 3, TOK, HEAD), B16),
        scratch_shapes=[pltpu.VMEM((HEAD, LENGTH), F32)],
        compiler_params=params(),
        cost_estimate=cost(10 * LENGTH * LENGTH * HEAD, 4 << 20, LENGTH * LENGTH // 2),
        name="attention_backward",
    )(x, stat)


def project_kernel(o_ref, w_ref, out_ref, lhs_ref):
    @pl.when(pl.program_id(0) == 0)
    def _():
        for h in range(HEADS):
            lhs_ref[:, h * HEAD : (h + 1) * HEAD] = o_ref[h]

    out_ref[...] = nn(lhs_ref[...], w_ref[...]).astype(B16)


def project(o, w):
    cols = 256
    return pl.pallas_call(
        project_kernel,
        grid=(WIDTH // cols,),
        in_specs=[
            pl.BlockSpec((HEADS, TOK, HEAD), lambda i: (0, 0, 0)),
            pl.BlockSpec((WIDTH, cols), lambda i: (0, i)),
        ],
        out_specs=pl.BlockSpec((TOK, cols), lambda i: (0, i)),
        out_shape=jax.ShapeDtypeStruct((TOK, WIDTH), B16),
        scratch_shapes=[pltpu.VMEM((TOK, WIDTH), B16)],
        compiler_params=params(),
        cost_estimate=cost(2 * TOK * WIDTH * WIDTH, 9 << 20),
        name="project",
    )(o, w)


def unpack_kernel(x_ref, q_ref, k_ref, v_ref):
    for h in range(4):
        cols = slice(h * HEAD, (h + 1) * HEAD)
        q_ref[:, cols] = x_ref[h, 0]
        k_ref[:, cols] = x_ref[h, 1]
        v_ref[:, cols] = x_ref[h, 2]


def unpack(x):
    shape = jax.ShapeDtypeStruct((TOK, WIDTH), B16)
    spec = pl.BlockSpec((TOK, 4 * HEAD), lambda i: (0, i))
    return pl.pallas_call(
        unpack_kernel,
        grid=(HEADS // 4,),
        in_specs=[pl.BlockSpec((4, 3, TOK, HEAD), lambda i: (i, 0, 0, 0))],
        out_specs=[spec, spec, spec],
        out_shape=[shape, shape, shape],
        compiler_params=params(),
        cost_estimate=cost(0, 3 << 20),
        name="unpack",
    )(x)


def seq_move(x, dz, dx, dc):
    pairs = []
    for z in range(ZN):
        for a in range(XN):
            for c in range(CN):
                source = (z * XN + a) * CN + c
                target = ((z + dz) % ZN * XN + (a + dx) % XN) * CN + (c + dc) % CN
                pairs.append((source, target))
    return lax.ppermute(x, "seq", pairs)


def dp_move(x, dh, dy):
    pairs = []
    for h in range(HN):
        for y in range(YN):
            pairs.append((h * YN + y, (h + dh) % HN * YN + (y + dy) % YN))
    return lax.ppermute(x, "dp", pairs)


def gather_grads(g):
    left = seq_move(g, 0, 1, 0)
    right = seq_move(g, 0, -1, 0)
    over = seq_move(g, 1, 0, 0)
    half = TOK // 2
    far_a = seq_move(left[:half], 0, 1, 0)
    far_b = seq_move(right[half:], 0, -1, 0)
    over_left = seq_move(over, 0, 1, 0)
    over_right = seq_move(over, 0, -1, 0)
    over_far_a = seq_move(far_a, 1, 0, 0)
    over_far_b = seq_move(far_b, 1, 0, 0)
    return [
        (0, 0, 0, g),
        (0, 3, 0, left),
        (0, 1, 0, right),
        (1, 0, 0, over),
        (0, 2, 0, far_a),
        (0, 2, half, far_b),
        (1, 3, 0, over_left),
        (1, 1, 0, over_right),
        (1, 2, 0, over_far_a),
        (1, 2, half, over_far_b),
    ]


def weight_kernel(places, pos_ref, keep_ref, got_ref, *refs):
    parts = refs[: len(places)]
    own_ref, other_ref, lhs_ref = refs[len(places) :]

    @pl.when(pl.program_id(0) == 0)
    def _():
        at = 0
        for dz, dx, first, rows in places:
            z = lax.rem(pos_ref[0] + dz, ZN)
            a = lax.rem(pos_ref[1] + dx, XN)
            index = z * XN + a
            lhs_ref[:HEAD, at : at + rows] = keep_ref[index][:, first : first + rows]
            lhs_ref[HEAD:, at : at + rows] = got_ref[index][:, first : first + rows]
            at += rows

    rhs = jnp.concatenate([part[...] for part in parts], axis=0)
    total = nn(lhs_ref[...], rhs)
    own_ref[...] = total[:HEAD]
    other_ref[...] = total[HEAD:].astype(B16)


def weight_partial(pos, keep, got, blocks):
    cols = 256
    places = [(dz, dx, first, a.shape[0]) for dz, dx, first, a in blocks]
    arrays = [a for _, _, _, a in blocks]

    def body(*refs):
        weight_kernel(places, *refs)

    whole = pl.BlockSpec((BLOCKS, HEAD, TOK), lambda i: (0, 0, 0))
    spec = pl.BlockSpec((HEAD, cols), lambda i: (0, i))
    return pl.pallas_call(
        body,
        grid=(WIDTH // cols,),
        in_specs=[pl.BlockSpec(memory_space=pltpu.SMEM), whole, whole]
        + [pl.BlockSpec((a.shape[0], cols), lambda i: (0, i)) for a in arrays],
        out_specs=[spec, spec],
        out_shape=[
            jax.ShapeDtypeStruct((HEAD, WIDTH), F32),
            jax.ShapeDtypeStruct((HEAD, WIDTH), B16),
        ],
        scratch_shapes=[pltpu.VMEM((2 * HEAD, LENGTH // 2), B16)],
        compiler_params=params(),
        cost_estimate=cost(2 * LENGTH * HEAD * WIDTH, 6 << 20),
        name="weight_partial",
    )(pos, keep, got, *arrays)


SHARE = HEAD // YN


def split_kernel(pos_ref, own_ref, got_ref, mine_ref, one_ref, two_ref, three_ref):
    y = pos_ref[3]
    for r, ref in enumerate((mine_ref, one_ref, two_ref, three_ref)):
        first = pl.multiple_of(lax.rem(y + r, YN) * SHARE, SHARE)
        rows = pl.ds(first, SHARE)
        ref[...] = (own_ref[rows, :] + got_ref[rows, :].astype(F32)).astype(ref.dtype)


def split_shares(pos, own, got):
    vmem = pl.BlockSpec(memory_space=pltpu.VMEM)
    return pl.pallas_call(
        split_kernel,
        in_specs=[pl.BlockSpec(memory_space=pltpu.SMEM), vmem, vmem],
        out_specs=[vmem] * 4,
        out_shape=[jax.ShapeDtypeStruct((SHARE, WIDTH), F32)]
        + [jax.ShapeDtypeStruct((SHARE, WIDTH), B16)] * 3,
        compiler_params=params(),
        cost_estimate=cost(0, 2 << 20),
        name="split_shares",
    )(pos, own, got)


def join_kernel(pos_ref, mine_ref, one_ref, two_ref, three_ref, out_ref):
    y = pos_ref[3]
    for r, ref in enumerate((mine_ref, one_ref, two_ref, three_ref)):
        first = pl.multiple_of(lax.rem(y + YN - r, YN) * SHARE, SHARE)
        out_ref[pl.ds(first, SHARE), :] = ref[...].astype(F32)


def join_shares(pos, shares):
    vmem = pl.BlockSpec(memory_space=pltpu.VMEM)
    return pl.pallas_call(
        join_kernel,
        in_specs=[pl.BlockSpec(memory_space=pltpu.SMEM)] + [vmem] * 4,
        out_specs=vmem,
        out_shape=jax.ShapeDtypeStruct((HEAD, WIDTH), F32),
        compiler_params=params(),
        cost_estimate=cost(0, 2 << 20),
        name="join_shares",
    )(pos, *shares)


def sum_over_dp(pos, own, got):
    mine, one, two, three = split_shares(pos, own, got)
    total = (
        mine
        + dp_move(one, 0, 1).astype(F32)
        + dp_move(two, 0, 2).astype(F32)
        + dp_move(three, 0, 3).astype(F32)
    ).astype(B16)
    share = (total.astype(F32) + dp_move(total, 1, 0).astype(F32)).astype(B16)
    shares = [share] + [dp_move(share, 0, r) for r in range(1, YN)]
    return join_shares(pos, shares)


def to_heads(x):
    return lax.all_to_all(x, "seq", split_axis=0, concat_axis=0, tiled=True)


def on_device(queries, keys, values, out_weight, out_grad):
    s = lax.axis_index("seq")
    y = lax.rem(lax.axis_index("dp"), YN)
    pos = jnp.stack([s // (XN * CN), lax.rem(s // CN, XN), lax.rem(s, CN), y]).astype(jnp.int32)
    q, k, v, g = (a.reshape(TOK, WIDTH) for a in (queries, keys, values, out_grad))
    blocks = gather_grads(g)
    x = to_heads(pack(q, k, v, g, out_weight))
    o, keep, send, stat = forward(pos, x)
    o_tokens = to_heads(o)
    got = seq_move(send, 0, 0, 1)
    own, other = weight_partial(pos, keep, got, blocks)
    grads = backward(x, stat)
    grad_weight = sum_over_dp(pos, own, seq_move(other, 0, 0, 1))
    grad_q, grad_k, grad_v = unpack(to_heads(grads))
    layer_out = project(o_tokens, out_weight)
    shape = (1, TOK, WIDTH)
    return (
        layer_out.reshape(shape),
        grad_q.reshape(shape),
        grad_k.reshape(shape),
        grad_v.reshape(shape),
        grad_weight,
    )


def solution(mesh):
    tokens = P("dp", "seq", None)
    return jax.shard_map(
        on_device,
        mesh=mesh,
        in_specs=(tokens, tokens, tokens, P(), tokens),
        out_specs=(tokens, tokens, tokens, tokens, P("seq", None)),
        check_vma=False,
    )
```

```python
import math

import jax
import jax.numpy as jnp
from jax import lax
from jax.experimental import pallas as pl
from jax.experimental.pallas import tpu as pltpu
from jax.sharding import PartitionSpec as P

B16 = jnp.bfloat16
F32 = jnp.float32
HEAD = 128
TOK = 128
LENGTH = 2048
WIDTH = 2048
HEADS = 16
BLOCK = 256
BLOCKS = LENGTH // BLOCK
FACTOR = HEAD ** (-0.5)
FACTOR2 = FACTOR * math.log2(math.e)
BIG = 60 << 20
SMALL = 32 << 20
WIDE = 57 << 20

ZN, XN, CN, YN, HN = 2, 4, 2, 4, 2


def nt(a, b):
    return lax.dot_general(a, b, (((1,), (1,)), ((), ())), preferred_element_type=F32)


def nn(a, b):
    return lax.dot_general(a, b, (((1,), (0,)), ((), ())), preferred_element_type=F32)


def params(limit):
    return pltpu.CompilerParams(vmem_limit_bytes=limit)


def cost(flops, nbytes, exps=0):
    return pl.CostEstimate(flops=flops, bytes_accessed=nbytes, transcendentals=exps)


PACK_HEADS = 8


def pack_kernel(q_ref, k_ref, v_ref, g_ref, *refs):
    out_ref = refs[PACK_HEADS]
    for h in range(PACK_HEADS):
        cols = slice(h * HEAD, (h + 1) * HEAD)
        out_ref[h, 0] = q_ref[:, cols]
        out_ref[h, 1] = k_ref[:, cols]
        out_ref[h, 2] = v_ref[:, cols]
        out_ref[h, 3] = nt(g_ref[...], refs[h][...]).astype(B16)


def pack(q, k, v, g, w):
    part = pl.BlockSpec((TOK, PACK_HEADS * HEAD), lambda i: (0, i))
    return pl.pallas_call(
        pack_kernel,
        grid=(HEADS // PACK_HEADS,),
        in_specs=[part, part, part, pl.BlockSpec((TOK, WIDTH), lambda i: (0, 0))]
        + [
            pl.BlockSpec((HEAD, WIDTH), lambda i, h=h: (PACK_HEADS * i + h, 0))
            for h in range(PACK_HEADS)
        ],
        out_specs=pl.BlockSpec((PACK_HEADS, 4, TOK, HEAD), lambda i: (i, 0, 0, 0)),
        out_shape=jax.ShapeDtypeStruct((HEADS, 4, TOK, HEAD), B16),
        compiler_params=params(WIDE),
        cost_estimate=cost(2 * TOK * WIDTH * WIDTH, 12 << 20),
        name="pack",
    )(q, k, v, g, *[w] * PACK_HEADS)


def rows_of(ref, which, first, count):
    return jnp.concatenate(
        [ref[t, which] for t in range(first // TOK, (first + count) // TOK)], axis=0
    )


def mask_of():
    key = lax.broadcasted_iota(jnp.int32, (BLOCK, BLOCK), 0)
    query = lax.broadcasted_iota(jnp.int32, (BLOCK, BLOCK), 1)
    return query >= key


def forward_kernel(x_ref, o_ref, ot_ref, stat_ref, vt_ref):
    visible = mask_of()
    for t in range(HEADS):
        vt_ref[:, t * TOK : (t + 1) * TOK] = x_ref[t, 2].T
    for j in range(BLOCKS):
        first = j * BLOCK
        q = rows_of(x_ref, 0, first, BLOCK)
        tiles = []
        for i in range(j + 1):
            s = nt(rows_of(x_ref, 1, i * BLOCK, BLOCK), q) * FACTOR2
            tiles.append(jnp.where(visible, s, -1e30) if i == j else s)
        top = tiles[0]
        for s in tiles[1:]:
            top = jnp.maximum(top, s)
        top = jnp.max(top, axis=0, keepdims=True)
        total = None
        acc = None
        for i, s in enumerate(tiles):
            p = jnp.exp2(s - top)
            total = p if total is None else total + p
            term = nn(vt_ref[:, i * BLOCK : (i + 1) * BLOCK], p.astype(B16))
            acc = term if acc is None else acc + term
        total = jnp.sum(total, axis=0, keepdims=True)
        ot = acc * (1.0 / total)
        oc = ot.T.astype(B16)
        ob = ot.astype(B16)
        for t in range(2):
            rows = slice(t * TOK, (t + 1) * TOK)
            o_ref[2 * j + t] = oc[rows]
            ot_ref[2 * j + t] = ob[:, rows]
        stat_ref[0:1, first : first + BLOCK] = top + jnp.log2(total)


def forward(x):
    vmem = pl.BlockSpec(memory_space=pltpu.VMEM)
    return pl.pallas_call(
        forward_kernel,
        in_specs=[vmem],
        out_specs=[vmem, vmem, vmem],
        out_shape=[
            jax.ShapeDtypeStruct((HEADS, TOK, HEAD), B16),
            jax.ShapeDtypeStruct((HEADS, HEAD, TOK), B16),
            jax.ShapeDtypeStruct((8, LENGTH), F32),
        ],
        scratch_shapes=[pltpu.VMEM((HEAD, LENGTH), B16)],
        compiler_params=params(SMALL),
        cost_estimate=cost(0, 0),
        name="attention_forward",
    )(x)


def backward_kernel(x_ref, o_ref, ot_ref, stat_ref, out_ref, dqt_ref, delta_ref):
    visible = mask_of()
    dqt_ref[...] = jnp.zeros_like(dqt_ref)
    for t in range(HEADS):
        product = x_ref[t, 3].T.astype(F32) * ot_ref[t].astype(F32)
        delta_ref[0:1, t * TOK : (t + 1) * TOK] = jnp.sum(product, axis=0, keepdims=True)
    for i in range(BLOCKS):
        first = i * BLOCK
        k = rows_of(x_ref, 1, first, BLOCK)
        v = rows_of(x_ref, 2, first, BLOCK)
        kt = k.T
        dk = None
        dv = None
        for j in range(i, BLOCKS):
            cols = slice(j * BLOCK, (j + 1) * BLOCK)
            q = rows_of(x_ref, 0, j * BLOCK, BLOCK)
            d = rows_of(x_ref, 3, j * BLOCK, BLOCK)
            s = nt(k, q) * FACTOR2 - stat_ref[0:1, cols]
            if i == j:
                s = jnp.where(visible, s, -1e30)
            p = jnp.exp2(s)
            dp = nt(v, d) - delta_ref[0:1, cols]
            ds = (p * dp).astype(B16)
            term = nn(p.astype(B16), d)
            dv = term if dv is None else dv + term
            term = nn(ds, q)
            dk = term if dk is None else dk + term
            dqt_ref[:, cols] += nn(kt, ds)
        dk = (dk * FACTOR).astype(B16)
        dv = dv.astype(B16)
        for t in range(2):
            rows = slice(t * TOK, (t + 1) * TOK)
            out_ref[2 * i + t, 1] = dk[rows]
            out_ref[2 * i + t, 2] = dv[rows]
    for t in range(HEADS):
        part = dqt_ref[:, t * TOK : (t + 1) * TOK] * FACTOR
        out_ref[t, 0] = part.T.astype(B16)
        out_ref[t, 3] = o_ref[t]


def backward(x, o, ot, stat):
    vmem = pl.BlockSpec(memory_space=pltpu.VMEM)
    return pl.pallas_call(
        backward_kernel,
        in_specs=[vmem] * 4,
        out_specs=vmem,
        out_shape=jax.ShapeDtypeStruct((HEADS, 4, TOK, HEAD), B16),
        scratch_shapes=[pltpu.VMEM((HEAD, LENGTH), F32), pltpu.VMEM((8, LENGTH), F32)],
        compiler_params=params(SMALL),
        cost_estimate=cost(0, 0),
        name="attention_backward",
    )(x, o, ot, stat)


WEIGHT_PARTS = 4
FINISH_STEPS = 2


def finish_kernel(x_ref, o_ref, *refs):
    weights = refs[:WEIGHT_PARTS]
    y_ref, q_ref, k_ref, v_ref, lhs_ref = refs[WEIGHT_PARTS:]

    @pl.when(pl.program_id(0) == 0)
    def _():
        for h in range(HEADS):
            lhs_ref[:, h * HEAD : (h + 1) * HEAD] = o_ref[h, 0]

    for h in range(HEADS // FINISH_STEPS):
        cols = slice(h * HEAD, (h + 1) * HEAD)
        q_ref[:, cols] = x_ref[h, 0]
        k_ref[:, cols] = x_ref[h, 1]
        v_ref[:, cols] = x_ref[h, 2]
    w = jnp.concatenate([ref[...] for ref in weights], axis=0)
    y_ref[...] = nn(lhs_ref[...], w).astype(B16)


def finish(x, w):
    rows = WIDTH // WEIGHT_PARTS
    cols = WIDTH // FINISH_STEPS
    shape = jax.ShapeDtypeStruct((TOK, WIDTH), B16)
    spec = pl.BlockSpec((TOK, cols), lambda i: (0, i))
    return pl.pallas_call(
        finish_kernel,
        grid=(FINISH_STEPS,),
        in_specs=[
            pl.BlockSpec((HEADS // FINISH_STEPS, 3, TOK, HEAD), lambda i: (i, 0, 0, 0)),
            pl.BlockSpec((HEADS, 1, TOK, HEAD), lambda i: (0, 3, 0, 0)),
        ]
        + [pl.BlockSpec((rows, cols), lambda i, n=n: (n, i)) for n in range(WEIGHT_PARTS)],
        out_specs=[spec] * 4,
        out_shape=[shape] * 4,
        scratch_shapes=[pltpu.VMEM((TOK, WIDTH), B16)],
        compiler_params=params(WIDE),
        cost_estimate=cost(2 * TOK * WIDTH * WIDTH, 12 << 20),
        name="finish",
    )(x, x, *[w] * WEIGHT_PARTS)


PART = 512
SHARE = HEAD // YN
GROUP = [(0, 0), (0, 1), (1, 0), (1, 1)]


def move(x, dh=0, dy=0, dz=0, dx=0, dc=0):
    pairs = []
    for h in range(HN):
        for y in range(YN):
            for z in range(ZN):
                for a in range(XN):
                    for c in range(CN):
                        source = (((h * YN + y) * ZN + z) * XN + a) * CN + c
                        target = ((h + dh) % HN * YN + (y + dy) % YN) * ZN + (z + dz) % ZN
                        target = (target * XN + (a + dx) % XN) * CN + (c + dc) % CN
                        pairs.append((source, target))
    return lax.ppermute(x, ("dp", "seq"), pairs)


def part_of(pos_ref, dz, dc):
    return lax.rem(pos_ref[0] + dz, ZN) * CN + lax.rem(pos_ref[2] + dc, CN)


def cut_kernel(pos_ref, g_ref, *refs):
    for ref, (dz, dc) in zip(refs, GROUP):
        first = pl.multiple_of(part_of(pos_ref, dz, dc) * PART, PART)
        ref[...] = g_ref[:, pl.ds(first, PART)]


def cut(pos, g):
    vmem = pl.BlockSpec(memory_space=pltpu.VMEM)
    return pl.pallas_call(
        cut_kernel,
        in_specs=[pl.BlockSpec(memory_space=pltpu.SMEM), vmem],
        out_specs=[vmem] * 4,
        out_shape=[jax.ShapeDtypeStruct((TOK, PART), B16)] * 4,
        compiler_params=params(SMALL),
        cost_estimate=cost(0, 1 << 20),
        name="cut",
    )(pos, g)


def join_rows_kernel(a_ref, b_ref, c_ref, d_ref, out_ref):
    for n, ref in enumerate((a_ref, b_ref, c_ref, d_ref)):
        out_ref[n * TOK : (n + 1) * TOK] = ref[...]


def join_rows(parts):
    vmem = pl.BlockSpec(memory_space=pltpu.VMEM)
    return pl.pallas_call(
        join_rows_kernel,
        in_specs=[vmem] * 4,
        out_specs=vmem,
        out_shape=jax.ShapeDtypeStruct((4 * TOK, PART), B16),
        compiler_params=params(SMALL),
        cost_estimate=cost(0, 1 << 20),
        name="join_rows",
    )(*parts)


def stack(parts):
    def body(*refs):
        for n in range(XN):
            refs[XN][n * 4 * TOK : (n + 1) * 4 * TOK] = refs[n][...]

    vmem = pl.BlockSpec(memory_space=pltpu.VMEM)
    return pl.pallas_call(
        body,
        in_specs=[vmem] * XN,
        out_specs=vmem,
        out_shape=jax.ShapeDtypeStruct((LENGTH, PART), B16),
        compiler_params=params(SMALL),
        cost_estimate=cost(0, STACK_COST << 20),
        name="stack",
    )(*parts)


STACK_COST = 100


def weight_kernel(pos_ref, *refs):
    heads, rhs_ref, shares = refs[:4], refs[4], refs[5:9]
    lhs_ref, total_ref = refs[9:]
    for dx in range(XN):
        for n, (dz, dc) in enumerate(GROUP):
            z = lax.rem(pos_ref[0] + dz, ZN)
            x = lax.rem(pos_ref[1] + dx, XN)
            c = lax.rem(pos_ref[2] + dc, CN)
            block = (z * XN + x) * CN + c
            at = (dx * 4 + n) * TOK
            for m, ref in enumerate(heads):
                lhs_ref[m * HEAD : (m + 1) * HEAD, at : at + TOK] = ref[block]
    total_ref[...] = nn(lhs_ref[...], rhs_ref[...])
    y = pos_ref[3]
    for r, ref in enumerate(shares):
        first = lax.rem(y + r, YN) * SHARE
        for m in range(4):
            at = pl.multiple_of(m * HEAD + first, SHARE)
            ref[m] = total_ref[pl.ds(at, SHARE), :].astype(ref.dtype)


def weight_partial(pos, heads, rows):
    vmem = pl.BlockSpec(memory_space=pltpu.VMEM)
    shape = (4, SHARE, PART)
    return pl.pallas_call(
        weight_kernel,
        in_specs=[pl.BlockSpec(memory_space=pltpu.SMEM)] + [vmem] * 5,
        out_specs=[vmem] * 4,
        out_shape=[jax.ShapeDtypeStruct(shape, F32)]
        + [jax.ShapeDtypeStruct(shape, B16)] * 3,
        scratch_shapes=[pltpu.VMEM((4 * HEAD, LENGTH), B16), pltpu.VMEM((4 * HEAD, PART), F32)],
        compiler_params=params(SMALL),
        cost_estimate=cost(2 * LENGTH * HEAD * WIDTH, 5 << 20),
        name="weight_partial",
    )(pos, *heads, rows)


def sum_shares_kernel(mine_ref, a_ref, b_ref, c_ref, *out_refs):
    for m, ref in enumerate(out_refs):
        total = mine_ref[m] + a_ref[m].astype(F32)
        ref[...] = (total + b_ref[m].astype(F32) + c_ref[m].astype(F32)).astype(B16)


def sum_shares(mine, a, b, c):
    vmem = pl.BlockSpec(memory_space=pltpu.VMEM)
    return pl.pallas_call(
        sum_shares_kernel,
        in_specs=[vmem] * 4,
        out_specs=[vmem] * 4,
        out_shape=[jax.ShapeDtypeStruct((SHARE, PART), B16)] * 4,
        compiler_params=params(SMALL),
        cost_estimate=cost(0, 1 << 20),
        name="sum_shares",
    )(mine, a, b, c)


def row_kernel(pos_ref, *refs):
    out_ref = refs[8]
    for n, (dz, dc) in enumerate(GROUP):
        first = pl.multiple_of(part_of(pos_ref, dz, dc) * PART, PART)
        total = refs[n][...].astype(F32) + refs[4 + n][...].astype(F32)
        out_ref[:, pl.ds(first, PART)] = total.astype(B16)


def make_rows(pos, near, far):
    vmem = pl.BlockSpec(memory_space=pltpu.VMEM)
    return pl.pallas_call(
        row_kernel,
        in_specs=[pl.BlockSpec(memory_space=pltpu.SMEM)] + [vmem] * 8,
        out_specs=vmem,
        out_shape=jax.ShapeDtypeStruct((SHARE, WIDTH), B16),
        compiler_params=params(SMALL),
        cost_estimate=cost(0, 1 << 20),
        name="make_rows",
    )(pos, *near, *far)


def join_kernel(pos_ref, mine_ref, one_ref, two_ref, three_ref, out_ref):
    y = pos_ref[3]
    for r, ref in enumerate((mine_ref, one_ref, two_ref, three_ref)):
        first = pl.multiple_of(lax.rem(y + YN - r, YN) * SHARE, SHARE)
        out_ref[pl.ds(first, SHARE), :] = ref[...].astype(F32)


def join_shares(pos, shares):
    vmem = pl.BlockSpec(memory_space=pltpu.VMEM)
    return pl.pallas_call(
        join_kernel,
        in_specs=[pl.BlockSpec(memory_space=pltpu.SMEM)] + [vmem] * 4,
        out_specs=vmem,
        out_shape=jax.ShapeDtypeStruct((HEAD, WIDTH), F32),
        compiler_params=params(SMALL),
        cost_estimate=cost(0, 2 << 20),
        name="join_shares",
    )(pos, *shares)


def share_over_dp(pos, mine, one, two, three):
    totals = sum_shares(mine, move(one, dy=1), move(two, dy=2), move(three, dy=3))
    near, far = [], []
    for (dz, dc), total in zip(GROUP, totals):
        near.append(total if dz + dc == 0 else move(total, dz=dz, dc=dc))
        far.append(move(total, dh=1, dz=dz, dc=dc))
    share = make_rows(pos, near, far)
    return [share] + [move(share, dy=r) for r in range(1, YN)]


def to_heads(x):
    return lax.all_to_all(x, "seq", split_axis=0, concat_axis=0, tiled=True)


def tie(*arrays):
    return lax.optimization_barrier(arrays)


def on_device(queries, keys, values, out_weight, out_grad):
    s = lax.axis_index("seq")
    y = lax.rem(lax.axis_index("dp"), YN)
    pos = jnp.stack([s // (XN * CN), lax.rem(s // CN, XN), lax.rem(s, CN), y]).astype(jnp.int32)
    q, k, v, g = (a.reshape(TOK, WIDTH) for a in (queries, keys, values, out_grad))
    cuts = cut(pos, g)
    parts = [cuts[0]] + [move(cuts[n], dz=GROUP[n][0], dc=GROUP[n][1]) for n in range(1, 4)]
    packed, *parts = tie(pack(q, k, v, g, out_weight), *parts)
    rows = join_rows(parts)
    x = to_heads(packed)
    x, rows = tie(x, rows)
    rows_near, rows_before = move(rows, dx=-1), move(rows, dx=-3)
    rows_far = move(rows, dx=-2)
    o, ot, stat = forward(x)
    beside = move(ot, dc=1)
    over = move(ot, dz=1)
    grads = backward(x, o, ot, stat)
    rows_near, rows_before, rows_far, grads = tie(rows_near, rows_before, rows_far, grads)
    rows = stack([rows, rows_near, rows_far, rows_before])
    over, beside, rows = tie(over, beside, rows)
    heads = [ot, beside, over, move(over, dc=1)]
    shares = weight_partial(pos, heads, rows)
    grads, *shares = tie(grads, *shares)
    share = share_over_dp(pos, *shares)
    results = to_heads(grads)
    layer_out, grad_q, grad_k, grad_v = finish(results, out_weight)
    layer_out, *share = tie(layer_out, *share)
    grad_weight = join_shares(pos, share)
    shape = (1, TOK, WIDTH)
    return (
        layer_out.reshape(shape),
        grad_q.reshape(shape),
        grad_k.reshape(shape),
        grad_v.reshape(shape),
        grad_weight,
    )


def solution(mesh):
    tokens = P("dp", "seq", None)
    return jax.shard_map(
        on_device,
        mesh=mesh,
        in_specs=(tokens, tokens, tokens, P(), tokens),
        out_specs=(tokens, tokens, tokens, tokens, P("seq", None)),
        check_vma=False,
    )
```

```python
import math

import jax
import jax.numpy as jnp
from jax import lax
from jax.experimental import pallas as pl
from jax.experimental.pallas import tpu as pltpu
from jax.sharding import PartitionSpec as P

B16 = jnp.bfloat16
F32 = jnp.float32
HEAD = 128
TOK = 128
LENGTH = 2048
WIDTH = 2048
HEADS = 16
BLOCK = 256
BLOCKS = LENGTH // BLOCK
FACTOR = HEAD ** (-0.5)
FACTOR2 = FACTOR * math.log2(math.e)
BIG = 60 << 20
SMALL = 32 << 20
WIDE = 57 << 20

ZN, XN, CN, YN, HN = 2, 4, 2, 4, 2


def nt(a, b):
    return lax.dot_general(a, b, (((1,), (1,)), ((), ())), preferred_element_type=F32)


def nn(a, b):
    return lax.dot_general(a, b, (((1,), (0,)), ((), ())), preferred_element_type=F32)


def params(limit):
    return pltpu.CompilerParams(vmem_limit_bytes=limit)


def cost(flops, nbytes, exps=0):
    return pl.CostEstimate(flops=flops, bytes_accessed=nbytes, transcendentals=exps)


PACK_HEADS = 8


def pack_kernel(q_ref, k_ref, v_ref, g_ref, *refs):
    out_ref = refs[PACK_HEADS]
    for h in range(PACK_HEADS):
        cols = slice(h * HEAD, (h + 1) * HEAD)
        out_ref[h, 0] = q_ref[:, cols]
        out_ref[h, 1] = k_ref[:, cols]
        out_ref[h, 2] = v_ref[:, cols]
        out_ref[h, 3] = nt(g_ref[...], refs[h][...]).astype(B16)


def pack(q, k, v, g, w):
    part = pl.BlockSpec((TOK, PACK_HEADS * HEAD), lambda i: (0, i))
    return pl.pallas_call(
        pack_kernel,
        grid=(HEADS // PACK_HEADS,),
        in_specs=[part, part, part, pl.BlockSpec((TOK, WIDTH), lambda i: (0, 0))]
        + [
            pl.BlockSpec((HEAD, WIDTH), lambda i, h=h: (PACK_HEADS * i + h, 0))
            for h in range(PACK_HEADS)
        ],
        out_specs=pl.BlockSpec((PACK_HEADS, 4, TOK, HEAD), lambda i: (i, 0, 0, 0)),
        out_shape=jax.ShapeDtypeStruct((HEADS, 4, TOK, HEAD), B16),
        compiler_params=params(WIDE),
        cost_estimate=cost(2 * TOK * WIDTH * WIDTH, 12 << 20),
        name="pack",
    )(q, k, v, g, *[w] * PACK_HEADS)


def rows_of(ref, which, first, count):
    return jnp.concatenate(
        [ref[t, which] for t in range(first // TOK, (first + count) // TOK)], axis=0
    )


def mask_of():
    key = lax.broadcasted_iota(jnp.int32, (BLOCK, BLOCK), 0)
    query = lax.broadcasted_iota(jnp.int32, (BLOCK, BLOCK), 1)
    return query >= key


def forward_kernel(x_ref, o_ref, ot_ref, stat_ref, vt_ref):
    visible = mask_of()
    for t in range(HEADS):
        vt_ref[:, t * TOK : (t + 1) * TOK] = x_ref[t, 2].T
    for j in range(BLOCKS):
        first = j * BLOCK
        q = rows_of(x_ref, 0, first, BLOCK)
        tiles = []
        for i in range(j + 1):
            s = nt(rows_of(x_ref, 1, i * BLOCK, BLOCK), q) * FACTOR2
            tiles.append(jnp.where(visible, s, -1e30) if i == j else s)
        top = tiles[0]
        for s in tiles[1:]:
            top = jnp.maximum(top, s)
        top = jnp.max(top, axis=0, keepdims=True)
        total = None
        acc = None
        for i, s in enumerate(tiles):
            p = jnp.exp2(s - top)
            total = p if total is None else total + p
            term = nn(vt_ref[:, i * BLOCK : (i + 1) * BLOCK], p.astype(B16))
            acc = term if acc is None else acc + term
        total = jnp.sum(total, axis=0, keepdims=True)
        ot = acc * (1.0 / total)
        oc = ot.T.astype(B16)
        ob = ot.astype(B16)
        for t in range(2):
            rows = slice(t * TOK, (t + 1) * TOK)
            o_ref[2 * j + t] = oc[rows]
            ot_ref[2 * j + t] = ob[:, rows]
        stat_ref[0:1, first : first + BLOCK] = top + jnp.log2(total)


def forward(x):
    vmem = pl.BlockSpec(memory_space=pltpu.VMEM)
    return pl.pallas_call(
        forward_kernel,
        in_specs=[vmem],
        out_specs=[vmem, vmem, vmem],
        out_shape=[
            jax.ShapeDtypeStruct((HEADS, TOK, HEAD), B16),
            jax.ShapeDtypeStruct((HEADS, HEAD, TOK), B16),
            jax.ShapeDtypeStruct((8, LENGTH), F32),
        ],
        scratch_shapes=[pltpu.VMEM((HEAD, LENGTH), B16)],
        compiler_params=params(SMALL),
        cost_estimate=cost(0, 0),
        name="attention_forward",
    )(x)


def backward_kernel(x_ref, o_ref, ot_ref, stat_ref, out_ref, dqt_ref, delta_ref):
    visible = mask_of()
    dqt_ref[...] = jnp.zeros_like(dqt_ref)
    for t in range(HEADS):
        product = x_ref[t, 3].T.astype(F32) * ot_ref[t].astype(F32)
        delta_ref[0:1, t * TOK : (t + 1) * TOK] = jnp.sum(product, axis=0, keepdims=True)
    for i in range(BLOCKS):
        first = i * BLOCK
        k = rows_of(x_ref, 1, first, BLOCK)
        v = rows_of(x_ref, 2, first, BLOCK)
        kt = k.T
        dk = None
        dv = None
        for j in range(i, BLOCKS):
            cols = slice(j * BLOCK, (j + 1) * BLOCK)
            q = rows_of(x_ref, 0, j * BLOCK, BLOCK)
            d = rows_of(x_ref, 3, j * BLOCK, BLOCK)
            s = nt(k, q) * FACTOR2 - stat_ref[0:1, cols]
            if i == j:
                s = jnp.where(visible, s, -1e30)
            p = jnp.exp2(s)
            dp = nt(v, d) - delta_ref[0:1, cols]
            ds = (p * dp).astype(B16)
            term = nn(p.astype(B16), d)
            dv = term if dv is None else dv + term
            term = nn(ds, q)
            dk = term if dk is None else dk + term
            dqt_ref[:, cols] += nn(kt, ds)
        dk = (dk * FACTOR).astype(B16)
        dv = dv.astype(B16)
        for t in range(2):
            rows = slice(t * TOK, (t + 1) * TOK)
            out_ref[2 * i + t, 1] = dk[rows]
            out_ref[2 * i + t, 2] = dv[rows]
    for t in range(HEADS):
        part = dqt_ref[:, t * TOK : (t + 1) * TOK] * FACTOR
        out_ref[t, 0] = part.T.astype(B16)
        out_ref[t, 3] = o_ref[t]


def backward(x, o, ot, stat):
    vmem = pl.BlockSpec(memory_space=pltpu.VMEM)
    return pl.pallas_call(
        backward_kernel,
        in_specs=[vmem] * 4,
        out_specs=vmem,
        out_shape=jax.ShapeDtypeStruct((HEADS, 4, TOK, HEAD), B16),
        scratch_shapes=[pltpu.VMEM((HEAD, LENGTH), F32), pltpu.VMEM((8, LENGTH), F32)],
        compiler_params=params(SMALL),
        cost_estimate=cost(0, 0),
        name="attention_backward",
    )(x, o, ot, stat)


WEIGHT_PARTS = 4
FINISH_STEPS = 2


def finish_kernel(x_ref, o_ref, *refs):
    weights = refs[:WEIGHT_PARTS]
    y_ref, q_ref, k_ref, v_ref, lhs_ref = refs[WEIGHT_PARTS:]

    @pl.when(pl.program_id(0) == 0)
    def _():
        for h in range(HEADS):
            lhs_ref[:, h * HEAD : (h + 1) * HEAD] = o_ref[h, 0]

    for h in range(HEADS // FINISH_STEPS):
        cols = slice(h * HEAD, (h + 1) * HEAD)
        q_ref[:, cols] = x_ref[h, 0]
        k_ref[:, cols] = x_ref[h, 1]
        v_ref[:, cols] = x_ref[h, 2]
    w = jnp.concatenate([ref[...] for ref in weights], axis=0)
    y_ref[...] = nn(lhs_ref[...], w).astype(B16)


def finish(x, w):
    rows = WIDTH // WEIGHT_PARTS
    cols = WIDTH // FINISH_STEPS
    shape = jax.ShapeDtypeStruct((TOK, WIDTH), B16)
    spec = pl.BlockSpec((TOK, cols), lambda i: (0, i))
    return pl.pallas_call(
        finish_kernel,
        grid=(FINISH_STEPS,),
        in_specs=[
            pl.BlockSpec((HEADS // FINISH_STEPS, 3, TOK, HEAD), lambda i: (i, 0, 0, 0)),
            pl.BlockSpec((HEADS, 1, TOK, HEAD), lambda i: (0, 3, 0, 0)),
        ]
        + [pl.BlockSpec((rows, cols), lambda i, n=n: (n, i)) for n in range(WEIGHT_PARTS)],
        out_specs=[spec] * 4,
        out_shape=[shape] * 4,
        scratch_shapes=[pltpu.VMEM((TOK, WIDTH), B16)],
        compiler_params=params(53 << 20),
        cost_estimate=cost(2 * TOK * WIDTH * WIDTH, 12 << 20),
        name="finish",
    )(x, x, *[w] * WEIGHT_PARTS)


PART = 512
SHARE = HEAD // YN
GROUP = [(0, 0), (0, 1), (1, 0), (1, 1)]


def move(x, dh=0, dy=0, dz=0, dx=0, dc=0):
    pairs = []
    for h in range(HN):
        for y in range(YN):
            for z in range(ZN):
                for a in range(XN):
                    for c in range(CN):
                        source = (((h * YN + y) * ZN + z) * XN + a) * CN + c
                        target = ((h + dh) % HN * YN + (y + dy) % YN) * ZN + (z + dz) % ZN
                        target = (target * XN + (a + dx) % XN) * CN + (c + dc) % CN
                        pairs.append((source, target))
    return lax.ppermute(x, ("dp", "seq"), pairs)


def part_of(pos_ref, dz, dc):
    return lax.rem(pos_ref[0] + dz, ZN) * CN + lax.rem(pos_ref[2] + dc, CN)


def cut_kernel(pos_ref, g_ref, *refs):
    for ref, (dz, dc) in zip(refs, GROUP):
        first = pl.multiple_of(part_of(pos_ref, dz, dc) * PART, PART)
        ref[...] = g_ref[:, pl.ds(first, PART)]


def cut(pos, g):
    vmem = pl.BlockSpec(memory_space=pltpu.VMEM)
    return pl.pallas_call(
        cut_kernel,
        in_specs=[pl.BlockSpec(memory_space=pltpu.SMEM), vmem],
        out_specs=[vmem] * 4,
        out_shape=[jax.ShapeDtypeStruct((TOK, PART), B16)] * 4,
        compiler_params=params(SMALL),
        cost_estimate=cost(0, 1 << 20),
        name="cut",
    )(pos, g)


def join_rows_kernel(a_ref, b_ref, c_ref, d_ref, out_ref):
    for n, ref in enumerate((a_ref, b_ref, c_ref, d_ref)):
        out_ref[n * TOK : (n + 1) * TOK] = ref[...]


def join_rows(parts):
    vmem = pl.BlockSpec(memory_space=pltpu.VMEM)
    return pl.pallas_call(
        join_rows_kernel,
        in_specs=[vmem] * 4,
        out_specs=vmem,
        out_shape=jax.ShapeDtypeStruct((4 * TOK, PART), B16),
        compiler_params=params(SMALL),
        cost_estimate=cost(0, 1 << 20),
        name="join_rows",
    )(*parts)


def stack(parts):
    def body(*refs):
        for n in range(XN):
            refs[XN][n * 4 * TOK : (n + 1) * 4 * TOK] = refs[n][...]

    vmem = pl.BlockSpec(memory_space=pltpu.VMEM)
    return pl.pallas_call(
        body,
        in_specs=[vmem] * XN,
        out_specs=vmem,
        out_shape=jax.ShapeDtypeStruct((LENGTH, PART), B16),
        compiler_params=params(SMALL),
        cost_estimate=cost(0, STACK_COST << 20),
        name="stack",
    )(*parts)


STACK_COST = 100


def weight_kernel(pos_ref, *refs):
    heads, rhs_ref, shares = refs[:4], refs[4], refs[5:9]
    lhs_ref, total_ref = refs[9:]
    for dx in range(XN):
        for n, (dz, dc) in enumerate(GROUP):
            z = lax.rem(pos_ref[0] + dz, ZN)
            x = lax.rem(pos_ref[1] + dx, XN)
            c = lax.rem(pos_ref[2] + dc, CN)
            block = (z * XN + x) * CN + c
            at = (dx * 4 + n) * TOK
            for m, ref in enumerate(heads):
                lhs_ref[m * HEAD : (m + 1) * HEAD, at : at + TOK] = ref[block]
    total_ref[...] = nn(lhs_ref[...], rhs_ref[...])
    y = pos_ref[3]
    for r, ref in enumerate(shares):
        first = lax.rem(y + r, YN) * SHARE
        for m in range(4):
            at = pl.multiple_of(m * HEAD + first, SHARE)
            ref[m] = total_ref[pl.ds(at, SHARE), :].astype(ref.dtype)


def weight_partial(pos, heads, rows):
    vmem = pl.BlockSpec(memory_space=pltpu.VMEM)
    shape = (4, SHARE, PART)
    return pl.pallas_call(
        weight_kernel,
        in_specs=[pl.BlockSpec(memory_space=pltpu.SMEM)] + [vmem] * 5,
        out_specs=[vmem] * 4,
        out_shape=[jax.ShapeDtypeStruct(shape, F32)]
        + [jax.ShapeDtypeStruct(shape, B16)] * 3,
        scratch_shapes=[pltpu.VMEM((4 * HEAD, LENGTH), B16), pltpu.VMEM((4 * HEAD, PART), F32)],
        compiler_params=params(SMALL),
        cost_estimate=cost(2 * LENGTH * HEAD * WIDTH, 5 << 20),
        name="weight_partial",
    )(pos, *heads, rows)


def sum_shares_kernel(mine_ref, a_ref, b_ref, c_ref, here_ref, over_ref):
    for m in range(4):
        total = mine_ref[m] + a_ref[m].astype(F32)
        total = (total + b_ref[m].astype(F32) + c_ref[m].astype(F32)).astype(B16)
        if m < 2:
            here_ref[m] = total
        else:
            over_ref[m - 2] = total


def sum_shares(mine, a, b, c):
    vmem = pl.BlockSpec(memory_space=pltpu.VMEM)
    return pl.pallas_call(
        sum_shares_kernel,
        in_specs=[vmem] * 4,
        out_specs=[vmem] * 2,
        out_shape=[jax.ShapeDtypeStruct((2, SHARE, PART), B16)] * 2,
        compiler_params=params(SMALL),
        cost_estimate=cost(0, 1 << 20),
        name="sum_shares",
    )(mine, a, b, c)


def sum_pairs_kernel(a_ref, a2_ref, b_ref, b2_ref, *out_refs):
    for m, ref in enumerate(out_refs):
        ref[0] = (a_ref[m].astype(F32) + a2_ref[m].astype(F32)).astype(B16)
        ref[1] = (b_ref[m].astype(F32) + b2_ref[m].astype(F32)).astype(B16)


def sum_pairs(a, a2, b, b2):
    vmem = pl.BlockSpec(memory_space=pltpu.VMEM)
    return pl.pallas_call(
        sum_pairs_kernel,
        in_specs=[vmem] * 4,
        out_specs=[vmem] * 2,
        out_shape=[jax.ShapeDtypeStruct((2, SHARE, PART), B16)] * 2,
        compiler_params=params(SMALL),
        cost_estimate=cost(0, 1 << 20),
        name="sum_pairs",
    )(a, a2, b, b2)


def row_kernel(pos_ref, mine_ref, got_ref, out_ref):
    for dz, dc in GROUP:
        first = pl.multiple_of(part_of(pos_ref, dz, dc) * PART, PART)
        out_ref[:, pl.ds(first, PART)] = got_ref[dz] if dc else mine_ref[dz]


def make_rows(pos, mine, got):
    vmem = pl.BlockSpec(memory_space=pltpu.VMEM)
    return pl.pallas_call(
        row_kernel,
        in_specs=[pl.BlockSpec(memory_space=pltpu.SMEM)] + [vmem] * 2,
        out_specs=vmem,
        out_shape=jax.ShapeDtypeStruct((SHARE, WIDTH), B16),
        compiler_params=params(SMALL),
        cost_estimate=cost(0, 1 << 20),
        name="make_rows",
    )(pos, mine, got)


def join_kernel(pos_ref, mine_ref, one_ref, two_ref, three_ref, out_ref):
    y = pos_ref[3]
    for r, ref in enumerate((mine_ref, one_ref, two_ref, three_ref)):
        first = pl.multiple_of(lax.rem(y + YN - r, YN) * SHARE, SHARE)
        out_ref[pl.ds(first, SHARE), :] = ref[...].astype(F32)


def join_shares(pos, shares):
    vmem = pl.BlockSpec(memory_space=pltpu.VMEM)
    return pl.pallas_call(
        join_kernel,
        in_specs=[pl.BlockSpec(memory_space=pltpu.SMEM)] + [vmem] * 4,
        out_specs=vmem,
        out_shape=jax.ShapeDtypeStruct((HEAD, WIDTH), F32),
        compiler_params=params(SMALL),
        cost_estimate=cost(0, 2 << 20),
        name="join_shares",
    )(pos, *shares)


def share_over_dp(pos, mine, one, two, three):
    here, over = sum_shares(mine, move(one, dy=1), move(two, dy=2), move(three, dy=3))
    own, other = sum_pairs(
        here, move(here, dh=1), move(over, dz=1), move(over, dh=1, dz=1)
    )
    share = make_rows(pos, own, move(other, dc=1))
    return [share] + [move(share, dy=r) for r in range(1, YN)]


def to_heads(x):
    return lax.all_to_all(x, "seq", split_axis=0, concat_axis=0, tiled=True)


def tie(*arrays):
    return lax.optimization_barrier(arrays)


def on_device(queries, keys, values, out_weight, out_grad):
    s = lax.axis_index("seq")
    y = lax.rem(lax.axis_index("dp"), YN)
    pos = jnp.stack([s // (XN * CN), lax.rem(s // CN, XN), lax.rem(s, CN), y]).astype(jnp.int32)
    q, k, v, g = (a.reshape(TOK, WIDTH) for a in (queries, keys, values, out_grad))
    cuts = cut(pos, g)
    parts = [cuts[0]] + [move(cuts[n], dz=GROUP[n][0], dc=GROUP[n][1]) for n in range(1, 4)]
    packed, *parts = tie(pack(q, k, v, g, out_weight), *parts)
    rows = join_rows(parts)
    x = to_heads(packed)
    x, rows = tie(x, rows)
    rows_near, rows_before = move(rows, dx=-1), move(rows, dx=-3)
    rows_far = move(rows, dx=-2)
    o, ot, stat = forward(x)
    beside = move(ot, dc=1)
    over = move(ot, dz=1)
    grads = backward(x, o, ot, stat)
    rows_near, rows_before, rows_far, grads = tie(rows_near, rows_before, rows_far, grads)
    rows = stack([rows, rows_near, rows_far, rows_before])
    over, beside, rows = tie(over, beside, rows)
    heads = [ot, beside, over, move(over, dc=1)]
    shares = weight_partial(pos, heads, rows)
    grads, *shares = tie(grads, *shares)
    share = share_over_dp(pos, *shares)
    results = to_heads(grads)
    layer_out, grad_q, grad_k, grad_v = finish(results, out_weight)
    layer_out, *share = tie(layer_out, *share)
    grad_weight = join_shares(pos, share)
    shape = (1, TOK, WIDTH)
    return (
        layer_out.reshape(shape),
        grad_q.reshape(shape),
        grad_k.reshape(shape),
        grad_v.reshape(shape),
        grad_weight,
    )


def solution(mesh):
    tokens = P("dp", "seq", None)
    return jax.shard_map(
        on_device,
        mesh=mesh,
        in_specs=(tokens, tokens, tokens, P(), tokens),
        out_specs=(tokens, tokens, tokens, tokens, P("seq", None)),
        check_vma=False,
    )
```

```python
import math

import jax
import jax.numpy as jnp
from jax import lax
from jax.experimental import pallas as pl
from jax.experimental.pallas import tpu as pltpu
from jax.sharding import PartitionSpec as P

B16 = jnp.bfloat16
F32 = jnp.float32
HEAD = 128
TOK = 128
LENGTH = 2048
WIDTH = 2048
HEADS = 16
BLOCK = 256
BLOCKS = LENGTH // BLOCK
FACTOR = HEAD ** (-0.5)
FACTOR2 = FACTOR * math.log2(math.e)
BIG = 60 << 20
SMALL = 32 << 20
WIDE = 57 << 20

ZN, XN, CN, YN, HN = 2, 4, 2, 4, 2


def nt(a, b):
    return lax.dot_general(a, b, (((1,), (1,)), ((), ())), preferred_element_type=F32)


def nn(a, b):
    return lax.dot_general(a, b, (((1,), (0,)), ((), ())), preferred_element_type=F32)


def params(limit):
    return pltpu.CompilerParams(vmem_limit_bytes=limit)


def cost(flops, nbytes, exps=0):
    return pl.CostEstimate(flops=flops, bytes_accessed=nbytes, transcendentals=exps)


PACK_HEADS = 8


def pack_kernel(q_ref, k_ref, v_ref, g_ref, *refs):
    out_ref = refs[PACK_HEADS]
    for h in range(PACK_HEADS):
        cols = slice(h * HEAD, (h + 1) * HEAD)
        out_ref[h, 0] = q_ref[:, cols]
        out_ref[h, 1] = k_ref[:, cols]
        out_ref[h, 2] = v_ref[:, cols]
        out_ref[h, 3] = nt(g_ref[...], refs[h][...]).astype(B16)


def pack(q, k, v, g, w):
    part = pl.BlockSpec((TOK, PACK_HEADS * HEAD), lambda i: (0, i))
    return pl.pallas_call(
        pack_kernel,
        grid=(HEADS // PACK_HEADS,),
        in_specs=[part, part, part, pl.BlockSpec((TOK, WIDTH), lambda i: (0, 0))]
        + [
            pl.BlockSpec((HEAD, WIDTH), lambda i, h=h: (PACK_HEADS * i + h, 0))
            for h in range(PACK_HEADS)
        ],
        out_specs=pl.BlockSpec((PACK_HEADS, 4, TOK, HEAD), lambda i: (i, 0, 0, 0)),
        out_shape=jax.ShapeDtypeStruct((HEADS, 4, TOK, HEAD), B16),
        compiler_params=params(WIDE),
        cost_estimate=cost(2 * TOK * WIDTH * WIDTH, 12 << 20),
        name="pack",
    )(q, k, v, g, *[w] * PACK_HEADS)


def rows_of(ref, which, first, count):
    return jnp.concatenate(
        [ref[t, which] for t in range(first // TOK, (first + count) // TOK)], axis=0
    )


def mask_of():
    key = lax.broadcasted_iota(jnp.int32, (BLOCK, BLOCK), 0)
    query = lax.broadcasted_iota(jnp.int32, (BLOCK, BLOCK), 1)
    return query >= key


def forward_kernel(x_ref, o_ref, ot_ref, stat_ref, vt_ref):
    visible = mask_of()
    for t in range(HEADS):
        vt_ref[:, t * TOK : (t + 1) * TOK] = x_ref[t, 2].T
    for j in range(BLOCKS):
        first = j * BLOCK
        q = rows_of(x_ref, 0, first, BLOCK)
        tiles = []
        for i in range(j + 1):
            s = nt(rows_of(x_ref, 1, i * BLOCK, BLOCK), q) * FACTOR2
            tiles.append(jnp.where(visible, s, -1e30) if i == j else s)
        top = tiles[0]
        for s in tiles[1:]:
            top = jnp.maximum(top, s)
        top = jnp.max(top, axis=0, keepdims=True)
        total = None
        acc = None
        for i, s in enumerate(tiles):
            p = jnp.exp2(s - top)
            total = p if total is None else total + p
            term = nn(vt_ref[:, i * BLOCK : (i + 1) * BLOCK], p.astype(B16))
            acc = term if acc is None else acc + term
        total = jnp.sum(total, axis=0, keepdims=True)
        ot = acc * (1.0 / total)
        oc = ot.T.astype(B16)
        ob = ot.astype(B16)
        for t in range(2):
            rows = slice(t * TOK, (t + 1) * TOK)
            o_ref[2 * j + t] = oc[rows]
            ot_ref[2 * j + t] = ob[:, rows]
        stat_ref[0:1, first : first + BLOCK] = top + jnp.log2(total)


def forward(x):
    vmem = pl.BlockSpec(memory_space=pltpu.VMEM)
    return pl.pallas_call(
        forward_kernel,
        in_specs=[vmem],
        out_specs=[vmem, vmem, vmem],
        out_shape=[
            jax.ShapeDtypeStruct((HEADS, TOK, HEAD), B16),
            jax.ShapeDtypeStruct((HEADS, HEAD, TOK), B16),
            jax.ShapeDtypeStruct((8, LENGTH), F32),
        ],
        scratch_shapes=[pltpu.VMEM((HEAD, LENGTH), B16)],
        compiler_params=params(SMALL),
        cost_estimate=cost(0, 0),
        name="attention_forward",
    )(x)


def backward_kernel(x_ref, o_ref, ot_ref, stat_ref, out_ref, dqt_ref, delta_ref):
    visible = mask_of()
    dqt_ref[...] = jnp.zeros_like(dqt_ref)
    for t in range(HEADS):
        product = x_ref[t, 3].T.astype(F32) * ot_ref[t].astype(F32)
        delta_ref[0:1, t * TOK : (t + 1) * TOK] = jnp.sum(product, axis=0, keepdims=True)
    for i in range(BLOCKS):
        first = i * BLOCK
        k = rows_of(x_ref, 1, first, BLOCK)
        v = rows_of(x_ref, 2, first, BLOCK)
        kt = k.T
        dk = None
        dv = None
        for j in range(i, BLOCKS):
            cols = slice(j * BLOCK, (j + 1) * BLOCK)
            q = rows_of(x_ref, 0, j * BLOCK, BLOCK)
            d = rows_of(x_ref, 3, j * BLOCK, BLOCK)
            s = nt(k, q) * FACTOR2 - stat_ref[0:1, cols]
            if i == j:
                s = jnp.where(visible, s, -1e30)
            p = jnp.exp2(s)
            dp = nt(v, d) - delta_ref[0:1, cols]
            ds = (p * dp).astype(B16)
            term = nn(p.astype(B16), d)
            dv = term if dv is None else dv + term
            term = nn(ds, q)
            dk = term if dk is None else dk + term
            dqt_ref[:, cols] += nn(kt, ds)
        dk = (dk * FACTOR).astype(B16)
        dv = dv.astype(B16)
        for t in range(2):
            rows = slice(t * TOK, (t + 1) * TOK)
            out_ref[2 * i + t, 1] = dk[rows]
            out_ref[2 * i + t, 2] = dv[rows]
    for t in range(HEADS):
        part = dqt_ref[:, t * TOK : (t + 1) * TOK] * FACTOR
        out_ref[t, 0] = part.T.astype(B16)
        out_ref[t, 3] = o_ref[t]


def backward(x, o, ot, stat):
    vmem = pl.BlockSpec(memory_space=pltpu.VMEM)
    return pl.pallas_call(
        backward_kernel,
        in_specs=[vmem] * 4,
        out_specs=vmem,
        out_shape=jax.ShapeDtypeStruct((HEADS, 4, TOK, HEAD), B16),
        scratch_shapes=[pltpu.VMEM((HEAD, LENGTH), F32), pltpu.VMEM((8, LENGTH), F32)],
        compiler_params=params(SMALL),
        cost_estimate=cost(0, 0),
        name="attention_backward",
    )(x, o, ot, stat)


WEIGHT_PARTS = 4
FINISH_STEPS = 2


def finish_kernel(x_ref, o_ref, *refs):
    weights = refs[:WEIGHT_PARTS]
    y_ref, q_ref, k_ref, v_ref, lhs_ref = refs[WEIGHT_PARTS:]

    @pl.when(pl.program_id(0) == 0)
    def _():
        for h in range(HEADS):
            lhs_ref[:, h * HEAD : (h + 1) * HEAD] = o_ref[h, 0]

    for h in range(HEADS // FINISH_STEPS):
        cols = slice(h * HEAD, (h + 1) * HEAD)
        q_ref[:, cols] = x_ref[h, 0]
        k_ref[:, cols] = x_ref[h, 1]
        v_ref[:, cols] = x_ref[h, 2]
    w = jnp.concatenate([ref[...] for ref in weights], axis=0)
    y_ref[...] = nn(lhs_ref[...], w).astype(B16)


def finish(x, w):
    rows = WIDTH // WEIGHT_PARTS
    cols = WIDTH // FINISH_STEPS
    shape = jax.ShapeDtypeStruct((TOK, WIDTH), B16)
    spec = pl.BlockSpec((TOK, cols), lambda i: (0, i))
    return pl.pallas_call(
        finish_kernel,
        grid=(FINISH_STEPS,),
        in_specs=[
            pl.BlockSpec((HEADS // FINISH_STEPS, 3, TOK, HEAD), lambda i: (i, 0, 0, 0)),
            pl.BlockSpec((HEADS, 1, TOK, HEAD), lambda i: (0, 3, 0, 0)),
        ]
        + [pl.BlockSpec((rows, cols), lambda i, n=n: (n, i)) for n in range(WEIGHT_PARTS)],
        out_specs=[spec] * 4,
        out_shape=[shape] * 4,
        scratch_shapes=[pltpu.VMEM((TOK, WIDTH), B16)],
        compiler_params=params(53 << 20),
        cost_estimate=cost(2 * TOK * WIDTH * WIDTH, 12 << 20),
        name="finish",
    )(x, x, *[w] * WEIGHT_PARTS)


PART = 512
SHARE = HEAD // YN
GROUP = [(0, 0), (0, 1), (1, 0), (1, 1)]


def move(x, dh=0, dy=0, dz=0, dx=0, dc=0):
    pairs = []
    for h in range(HN):
        for y in range(YN):
            for z in range(ZN):
                for a in range(XN):
                    for c in range(CN):
                        source = (((h * YN + y) * ZN + z) * XN + a) * CN + c
                        target = ((h + dh) % HN * YN + (y + dy) % YN) * ZN + (z + dz) % ZN
                        target = (target * XN + (a + dx) % XN) * CN + (c + dc) % CN
                        pairs.append((source, target))
    return lax.ppermute(x, ("dp", "seq"), pairs)


def part_of(pos_ref, dz, dc):
    return lax.rem(pos_ref[0] + dz, ZN) * CN + lax.rem(pos_ref[2] + dc, CN)


def cut_kernel(pos_ref, g_ref, *refs):
    for ref, (dz, dc) in zip(refs, GROUP):
        first = pl.multiple_of(part_of(pos_ref, dz, dc) * PART, PART)
        ref[...] = g_ref[:, pl.ds(first, PART)]


def cut(pos, g):
    vmem = pl.BlockSpec(memory_space=pltpu.VMEM)
    return pl.pallas_call(
        cut_kernel,
        in_specs=[pl.BlockSpec(memory_space=pltpu.SMEM), vmem],
        out_specs=[vmem] * 4,
        out_shape=[jax.ShapeDtypeStruct((TOK, PART), B16)] * 4,
        compiler_params=params(SMALL),
        cost_estimate=cost(0, 1 << 20),
        name="cut",
    )(pos, g)


def join_rows_kernel(a_ref, b_ref, c_ref, d_ref, out_ref):
    for n, ref in enumerate((a_ref, b_ref, c_ref, d_ref)):
        out_ref[n * TOK : (n + 1) * TOK] = ref[...]


def join_rows(parts):
    vmem = pl.BlockSpec(memory_space=pltpu.VMEM)
    return pl.pallas_call(
        join_rows_kernel,
        in_specs=[vmem] * 4,
        out_specs=vmem,
        out_shape=jax.ShapeDtypeStruct((4 * TOK, PART), B16),
        compiler_params=params(SMALL),
        cost_estimate=cost(0, 1 << 20),
        name="join_rows",
    )(*parts)


def stack(parts):
    def body(*refs):
        for n in range(XN):
            refs[XN][n * 4 * TOK : (n + 1) * 4 * TOK] = refs[n][...]

    vmem = pl.BlockSpec(memory_space=pltpu.VMEM)
    return pl.pallas_call(
        body,
        in_specs=[vmem] * XN,
        out_specs=vmem,
        out_shape=jax.ShapeDtypeStruct((LENGTH, PART), B16),
        compiler_params=params(SMALL),
        cost_estimate=cost(0, STACK_COST << 20),
        name="stack",
    )(*parts)


STACK_COST = 100


def weight_kernel(pos_ref, *refs):
    heads, rhs_ref, shares = refs[:4], refs[4], refs[5:9]
    lhs_ref, total_ref = refs[9:]
    for place, dx in enumerate((0, 2, 1, 3)):
        for n, (dz, dc) in enumerate(GROUP):
            z = lax.rem(pos_ref[0] + dz, ZN)
            x = lax.rem(pos_ref[1] + dx, XN)
            c = lax.rem(pos_ref[2] + dc, CN)
            block = (z * XN + x) * CN + c
            at = (place * 4 + n) * TOK
            for m, ref in enumerate(heads):
                lhs_ref[m * HEAD : (m + 1) * HEAD, at : at + TOK] = ref[block]
    total_ref[...] = nn(lhs_ref[...], rhs_ref[...])
    y = pos_ref[3]
    for r, ref in enumerate(shares):
        first = lax.rem(y + r, YN) * SHARE
        for m in range(4):
            at = pl.multiple_of(m * HEAD + first, SHARE)
            ref[m] = total_ref[pl.ds(at, SHARE), :].astype(ref.dtype)


def weight_partial(pos, heads, rows):
    vmem = pl.BlockSpec(memory_space=pltpu.VMEM)
    shape = (4, SHARE, PART)
    return pl.pallas_call(
        weight_kernel,
        in_specs=[pl.BlockSpec(memory_space=pltpu.SMEM)] + [vmem] * 5,
        out_specs=[vmem] * 4,
        out_shape=[jax.ShapeDtypeStruct(shape, F32)]
        + [jax.ShapeDtypeStruct(shape, B16)] * 3,
        scratch_shapes=[pltpu.VMEM((4 * HEAD, LENGTH), B16), pltpu.VMEM((4 * HEAD, PART), F32)],
        compiler_params=params(SMALL),
        cost_estimate=cost(2 * LENGTH * HEAD * WIDTH, 5 << 20),
        name="weight_partial",
    )(pos, *heads, rows)


def sum_shares_kernel(mine_ref, a_ref, b_ref, c_ref, here_ref, over_ref):
    for m in range(4):
        total = mine_ref[m] + a_ref[m].astype(F32)
        total = (total + b_ref[m].astype(F32) + c_ref[m].astype(F32)).astype(B16)
        if m < 2:
            here_ref[m] = total
        else:
            over_ref[m - 2] = total


def sum_shares(mine, a, b, c):
    vmem = pl.BlockSpec(memory_space=pltpu.VMEM)
    return pl.pallas_call(
        sum_shares_kernel,
        in_specs=[vmem] * 4,
        out_specs=[vmem] * 2,
        out_shape=[jax.ShapeDtypeStruct((2, SHARE, PART), B16)] * 2,
        compiler_params=params(SMALL),
        cost_estimate=cost(0, 1 << 20),
        name="sum_shares",
    )(mine, a, b, c)


def sum_pairs_kernel(a_ref, a2_ref, b_ref, b2_ref, *out_refs):
    for m, ref in enumerate(out_refs):
        ref[0] = (a_ref[m].astype(F32) + a2_ref[m].astype(F32)).astype(B16)
        ref[1] = (b_ref[m].astype(F32) + b2_ref[m].astype(F32)).astype(B16)


def sum_pairs(a, a2, b, b2):
    vmem = pl.BlockSpec(memory_space=pltpu.VMEM)
    return pl.pallas_call(
        sum_pairs_kernel,
        in_specs=[vmem] * 4,
        out_specs=[vmem] * 2,
        out_shape=[jax.ShapeDtypeStruct((2, SHARE, PART), B16)] * 2,
        compiler_params=params(SMALL),
        cost_estimate=cost(0, 1 << 20),
        name="sum_pairs",
    )(a, a2, b, b2)


def row_kernel(pos_ref, mine_ref, got_ref, out_ref):
    for dz, dc in GROUP:
        first = pl.multiple_of(part_of(pos_ref, dz, dc) * PART, PART)
        out_ref[:, pl.ds(first, PART)] = got_ref[dz] if dc else mine_ref[dz]


def make_rows(pos, mine, got):
    vmem = pl.BlockSpec(memory_space=pltpu.VMEM)
    return pl.pallas_call(
        row_kernel,
        in_specs=[pl.BlockSpec(memory_space=pltpu.SMEM)] + [vmem] * 2,
        out_specs=vmem,
        out_shape=jax.ShapeDtypeStruct((SHARE, WIDTH), B16),
        compiler_params=params(SMALL),
        cost_estimate=cost(0, 1 << 20),
        name="make_rows",
    )(pos, mine, got)


def join_kernel(pos_ref, mine_ref, one_ref, two_ref, three_ref, out_ref):
    y = pos_ref[3]
    for r, ref in enumerate((mine_ref, one_ref, two_ref, three_ref)):
        first = pl.multiple_of(lax.rem(y + YN - r, YN) * SHARE, SHARE)
        out_ref[pl.ds(first, SHARE), :] = ref[...].astype(F32)


def join_shares(pos, shares):
    vmem = pl.BlockSpec(memory_space=pltpu.VMEM)
    return pl.pallas_call(
        join_kernel,
        in_specs=[pl.BlockSpec(memory_space=pltpu.SMEM)] + [vmem] * 4,
        out_specs=vmem,
        out_shape=jax.ShapeDtypeStruct((HEAD, WIDTH), F32),
        compiler_params=params(SMALL),
        cost_estimate=cost(0, 2 << 20),
        name="join_shares",
    )(pos, *shares)


def share_over_dp(pos, mine, one, two, three):
    here, over = sum_shares(mine, move(one, dy=1), move(two, dy=2), move(three, dy=3))
    own, other = sum_pairs(
        here, move(here, dh=1), move(over, dz=1), move(over, dh=1, dz=1)
    )
    share = make_rows(pos, own, move(other, dc=1))
    return [share] + [move(share, dy=r) for r in range(1, YN)]


def to_heads(x):
    return lax.all_to_all(x, "seq", split_axis=0, concat_axis=0, tiled=True)


def tie(*arrays):
    return lax.optimization_barrier(arrays)


def on_device(queries, keys, values, out_weight, out_grad):
    s = lax.axis_index("seq")
    y = lax.rem(lax.axis_index("dp"), YN)
    pos = jnp.stack([s // (XN * CN), lax.rem(s // CN, XN), lax.rem(s, CN), y]).astype(jnp.int32)
    q, k, v, g = (a.reshape(TOK, WIDTH) for a in (queries, keys, values, out_grad))
    cuts = cut(pos, g)
    parts = [cuts[0]] + [move(cuts[n], dz=GROUP[n][0], dc=GROUP[n][1]) for n in range(1, 4)]
    packed, *parts = tie(pack(q, k, v, g, out_weight), *parts)
    rows = join_rows(parts)
    x = to_heads(packed)
    x, rows = tie(x, rows)
    rows_far = move(rows, dx=-2)
    rows_near, rows_before = move(rows, dx=-1), move(rows, dx=-3)
    o, ot, stat = forward(x)
    beside = move(ot, dc=1)
    over = move(ot, dz=1)
    grads = backward(x, o, ot, stat)
    rows_far, rows_near, rows_before, grads = tie(rows_far, rows_near, rows_before, grads)
    rows = stack([rows, rows_far, rows_near, rows_before])
    over, beside, rows = tie(over, beside, rows)
    heads = [ot, beside, over, move(over, dc=1)]
    shares = weight_partial(pos, heads, rows)
    grads, *shares = tie(grads, *shares)
    share = share_over_dp(pos, *shares)
    results = to_heads(grads)
    layer_out, grad_q, grad_k, grad_v = finish(results, out_weight)
    layer_out, *share = tie(layer_out, *share)
    grad_weight = join_shares(pos, share)
    shape = (1, TOK, WIDTH)
    return (
        layer_out.reshape(shape),
        grad_q.reshape(shape),
        grad_k.reshape(shape),
        grad_v.reshape(shape),
        grad_weight,
    )


def solution(mesh):
    tokens = P("dp", "seq", None)
    return jax.shard_map(
        on_device,
        mesh=mesh,
        in_specs=(tokens, tokens, tokens, P(), tokens),
        out_specs=(tokens, tokens, tokens, tokens, P("seq", None)),
        check_vma=False,
    )
```
